128 devices in a mesh: row: 16 (over x, z_lo, core), col: 8 (over y, z_hi).
Axes of the slice: x: 4, y: 4, z: 4 (z_hi: 2, z_lo: 2; z = z_hi * 2 + z_lo), core: 2. Of those that a mesh axis runs over, the one named last changes fastest.
Arguments:
- features: bfloat16 [32768, 512], P(('row', 'col')), may hold values from -6 to 6
- weight: bfloat16 [512, 512], replicated, may hold values from -0.25 to 0.25
- cotangent: bfloat16 [32768, 512], P(('col', 'row')), may hold values from -6 to 6
- tiles: bfloat16 [16, 8, 128, 128, 128], P('row', 'col'), may hold values from -0.09375 to 0.09375
- tile_rows: int32 [16, 8, 128], P('row', 'col'), may hold values from 0 to 31, as said below
- tile_cols: int32 [16, 8, 128], P('row', 'col'), may hold values from 0 to 15
- tile_count: int32 [16, 8, 1], P('row', 'col'), may hold values from 16 to 128, as said below
Outputs:
- activations: bfloat16 [32768, 512], P(('col', 'row'))
- weight_grad: float32 [512, 512], replicated
- feature_grad: bfloat16 [32768, 512], P(('row', 'col'))
The draws below stay inside these ranges and needn't reach their ends.
Inputs may be any that keep to these rules, and one draw needn't show every extreme that they name: Within one grid cell the live slots name distinct (tile_rows, tile_cols) pairs. `tile_count`: some grid cell holds 128 live tiles in every draw.
All inputs are finite; a program needn't handle non-finite values.
Results may differ from the reference program's by a relative error of at most 0.0065.
Values may be sent and summed in bfloat16 or wider, within the bound.
No kernel may reach another device: no remote copies, remote signals or barrier semaphores. Data moves between devices by JAX's collectives and lax.ppermute only.
A program may use at most 128 MiB of HBM per device.

```python
import jax
import jax.numpy as jnp
from jax import lax

HID = 512
BLOCK = 128
BLK_DEV = 2
TMAX = 128
ROW_BLOCKS = 32
COL_BLOCKS = 16
NODES = 32768
N_ROW = 16
N_COL = 8


def tile_positions(key):
    cell_keys = jax.random.split(key, N_ROW * N_COL)
    total_spots = ROW_BLOCKS * COL_BLOCKS

    def one_cell(cell_key):
        return jax.random.permutation(cell_key, total_spots)[:TMAX]
    chosen = jax.vmap(one_cell)(cell_keys)
    return chosen.reshape(N_ROW, N_COL, TMAX).astype(jnp.int32)


def draw_tile_rows(key, part):
    spots = tile_positions(key)
    return (spots // COL_BLOCKS).astype(jnp.int32)


def draw_tile_cols(key, part):
    spots = tile_positions(key)
    return (spots % COL_BLOCKS).astype(jnp.int32)


def draw_tile_count(key, part):
    key = jax.random.fold_in(key, 3)
    first_key, second_key = jax.random.split(key)
    shifts = jax.random.randint(first_key, (N_ROW * N_COL,), 0, 4)
    counts = jnp.right_shift(jnp.full((N_ROW * N_COL,), TMAX, jnp.int32), shifts.astype(jnp.int32))
    fullest = jax.random.randint(second_key, (), 0, N_ROW * N_COL)
    counts = jnp.where(jnp.arange(N_ROW * N_COL, dtype=jnp.int32) == fullest, TMAX, counts)
    return counts.reshape(N_ROW, N_COL, 1).astype(jnp.int32)


def block_levels(key, extent, cuts, smallest, largest):
    gain, own = 1.0, jax.random.fold_in(key, 6)
    for position, shards_of in cuts:
        draws = jnp.exp(jax.random.uniform(jax.random.fold_in(own, position), (shards_of,), jnp.float32, smallest / len(cuts), largest / len(cuts)))
        gain = gain * jnp.repeat(draws, extent[position] // shards_of).reshape([-1 if axis == position else 1 for axis in range(len(extent))])
    return gain


def centred(key, extent, deviation, bound, cuts=(), kind=jnp.bfloat16):
    factor_of = block_levels(key, extent, cuts, -0.22, 0.18) if cuts else 1.0
    array = jax.random.normal(key, extent, jnp.float32) * deviation * factor_of
    return jnp.minimum(jnp.maximum(array, -bound), bound).astype(kind)


def setup_inputs(seed: int = 0) -> dict:
    key_list = jax.random.split(jax.random.key(seed), 8)
    features = centred(key_list[0], (NODES, HID), 1.0, 6.0, ((0, 128),))
    weight = centred(key_list[1], (HID, HID), HID ** -0.5, 0.25)
    cotangent = centred(key_list[2], (NODES, HID), 1.0, 6.0, ((0, 128),))
    tiles = centred(key_list[3], (N_ROW, N_COL, TMAX, BLOCK, BLOCK), (TMAX * BLOCK // (2 * BLK_DEV)) ** -0.5, 0.09375, ((0, 16), (1, 8)))
    tile_rows = draw_tile_rows(jax.random.fold_in(key_list[7], 71), 0)
    tile_cols = draw_tile_cols(jax.random.fold_in(key_list[7], 71), 0)
    tile_count = draw_tile_count(jax.random.fold_in(key_list[7], 71), 0)
    return {"features": features, "weight": weight, "cotangent": cotangent, "tiles": tiles, "tile_rows": tile_rows, "tile_cols": tile_cols, "tile_count": tile_count}


def silu_slope(values):
    sigma = jax.nn.sigmoid(values)
    return sigma * (1.0 + values * (1.0 - sigma))


def reference(features, weight, cotangent, tiles, tile_rows, tile_cols, tile_count):
    width = weight.shape[0]
    side = tiles.shape[-1]
    row_blocks = BLK_DEV * N_ROW
    col_blocks = BLK_DEV * N_COL
    feat_blocks = features.reshape(N_ROW, col_blocks, side, width)
    slot_ids = jnp.arange(TMAX, dtype=jnp.int32)

    def forward_cell(running, dev_index):
        row_at = dev_index // N_COL
        col_at = dev_index % N_COL
        tile_set = tiles[row_at, col_at].astype(jnp.float32)
        live_mask = (slot_ids < tile_count[row_at, col_at, 0]).astype(jnp.float32)
        picked = feat_blocks[row_at][tile_cols[row_at, col_at]].astype(jnp.float32)
        product = jnp.einsum("tpq,tqf->tpf", tile_set, picked, precision=lax.Precision.HIGHEST)
        product = product * live_mask[:, None, None]
        partial_value = jnp.zeros((row_blocks, side, width), jnp.float32).at[tile_rows[row_at, col_at]].add(product)
        return running.at[col_at].add(partial_value), None

    start_fwd = jnp.zeros((N_COL, row_blocks, side, width), jnp.float32)
    summed, _ = lax.scan(forward_cell, start_fwd, jnp.arange(N_ROW * N_COL, dtype=jnp.int32))
    mixed_rows = summed.reshape(NODES, width).astype(jnp.bfloat16)
    pre_act = jnp.dot(mixed_rows, weight, preferred_element_type=jnp.float32)
    activations = jax.nn.silu(pre_act).astype(jnp.bfloat16)
    grad_pre = (cotangent.astype(jnp.float32) * silu_slope(pre_act)).astype(jnp.bfloat16)
    weight_grad = jnp.dot(mixed_rows.T, grad_pre, preferred_element_type=jnp.float32) * (NODES ** -0.5)
    grad_mixed = jnp.dot(grad_pre, weight.T, preferred_element_type=jnp.float32).astype(jnp.bfloat16)
    grad_blocks = grad_mixed.reshape(N_COL, row_blocks, side, width)

    def backward_cell(running, dev_index):
        row_at = dev_index // N_COL
        col_at = dev_index % N_COL
        tile_set = tiles[row_at, col_at].astype(jnp.float32)
        live_mask = (slot_ids < tile_count[row_at, col_at, 0]).astype(jnp.float32)
        picked = grad_blocks[col_at][tile_rows[row_at, col_at]].astype(jnp.float32)
        product = jnp.einsum("tpq,tpf->tqf", tile_set, picked, precision=lax.Precision.HIGHEST)
        product = product * live_mask[:, None, None]
        partial_value = jnp.zeros((col_blocks, side, width), jnp.float32).at[tile_cols[row_at, col_at]].add(product)
        return running.at[row_at].add(partial_value), None

    start_bwd = jnp.zeros((N_ROW, col_blocks, side, width), jnp.float32)
    back_sum, _ = lax.scan(backward_cell, start_bwd, jnp.arange(N_ROW * N_COL, dtype=jnp.int32))
    feature_grad = back_sum.reshape(NODES, width).astype(jnp.bfloat16)
    return (activations, weight_grad, feature_grad)
```

```python
import jax
import jax.numpy as jnp
from jax import lax
from jax.experimental import pallas as pl
from jax.experimental.pallas import tpu as pltpu
from jax.sharding import Mesh, PartitionSpec as P

BF = jnp.bfloat16
F32 = jnp.float32
CHUNK = 32
UNROLL = 16


def tile_sums(forward, counts, rows, cols, own, sib, source, out_blocks):
    slots, side, _ = own.shape
    width = source.shape[-1]
    turns = slots // CHUNK

    def kernel(counts, rows, cols, own, sib, source, out, total):
        step = pl.program_id(0)

        @pl.when(step == 0)
        def _():
            total[...] = jnp.zeros_like(total)

        def chunk_sums(which, held, chunk):
            live = jnp.clip(counts[which] - chunk * CHUNK, 0, CHUNK)

            def one(place, carry):
                slot = chunk * CHUNK + place
                r, c = rows[which, slot], cols[which, slot]
                if forward:
                    total[r] += jnp.dot(held[place], source[c], preferred_element_type=F32)
                else:
                    total[c] += lax.dot_general(
                        held[place], source[r], (((0,), (0,)), ((), ())), preferred_element_type=F32
                    )
                return carry

            def several(group, carry):
                for u in range(UNROLL):
                    one(group * UNROLL + u, 0)
                return carry

            full = live // UNROLL
            lax.fori_loop(0, full, several, 0)
            lax.fori_loop(full * UNROLL, live, one, 0)

        @pl.when(step < turns)
        def _():
            chunk_sums(0, own, step)

        @pl.when(step >= turns)
        def _():
            chunk_sums(1, sib, step - turns)

        @pl.when(step == 2 * turns - 1)
        def _():
            out[...] = total[...].astype(BF)

    def own_at(i, counts, *_):
        return (jnp.minimum(jnp.minimum(i, turns - 1), jnp.maximum(counts[0] - 1, 0) // CHUNK), 0, 0)

    def sib_at(i, counts, *_):
        return (jnp.minimum(jnp.maximum(i - turns, 0), jnp.maximum(counts[1] - 1, 0) // CHUNK), 0, 0)

    shape = (out_blocks, side, width)
    return pl.pallas_call(
        kernel,
        grid_spec=pltpu.PrefetchScalarGridSpec(
            num_scalar_prefetch=3,
            grid=(2 * turns,),
            in_specs=[
                pl.BlockSpec((CHUNK, side, side), own_at),
                pl.BlockSpec((CHUNK, side, side), sib_at),
                pl.BlockSpec(source.shape, lambda i, *_: (0, 0, 0)),
            ],
            out_specs=pl.BlockSpec(shape, lambda i, *_: (0, 0, 0)),
            scratch_shapes=[pltpu.VMEM(shape, F32)],
        ),
        out_shape=jax.ShapeDtypeStruct(shape, BF),
        compiler_params=pltpu.CompilerParams(
            vmem_limit_bytes=40 << 20, dimension_semantics=("arbitrary",)
        ),
        cost_estimate=pl.CostEstimate(
            flops=4 * slots * side * side * width, bytes_accessed=16 << 20, transcendentals=0
        ),
        name="forward_tiles" if forward else "backward_tiles",
    )(counts, rows, cols, own, sib, source)


def middle(parts, weight, cotangent):
    chips, cores, own_rows, half = parts.shape
    width = cores * half

    def kernel(parts, weight, cot, act, grad, wgrad):
        w = weight[...]
        mixed = jnp.concatenate(
            [jnp.sum(parts[:, s].astype(F32), axis=0).astype(BF) for s in range(cores)], axis=1
        )
        pre = jnp.dot(mixed, w, preferred_element_type=F32)
        sig = jax.nn.sigmoid(pre)
        act[...] = (pre * sig).astype(BF)
        slope = sig * (1.0 + pre * (1.0 - sig))
        grad_pre = (cot[...].astype(F32) * slope).astype(BF)
        wgrad[...] = lax.dot_general(
            mixed, grad_pre, (((0,), (0,)), ((), ())), preferred_element_type=F32
        )
        mixed_grad = lax.dot_general(
            grad_pre, w, (((1,), (1,)), ((), ())), preferred_element_type=F32
        ).astype(BF)
        for s in range(cores):
            piece = mixed_grad[:, s * half : (s + 1) * half]
            for chip in range(chips):
                grad[chip, s] = piece

    return pl.pallas_call(
        kernel,
        out_shape=(
            jax.ShapeDtypeStruct((own_rows, width), BF),
            jax.ShapeDtypeStruct(parts.shape, BF),
            jax.ShapeDtypeStruct((width, width), F32),
        ),
        compiler_params=pltpu.CompilerParams(vmem_limit_bytes=40 << 20),
        cost_estimate=pl.CostEstimate(
            flops=6 * own_rows * width * width, bytes_accessed=7 << 20, transcendentals=own_rows * width
        ),
        name="middle",
    )(parts, weight, cotangent)


def local(features, weight, cotangent, tiles, tile_rows, tile_cols, tile_count):
    slots, side = tiles.shape[2], tiles.shape[3]
    own_rows, width = features.shape
    cores = lax.axis_size("core")
    chips = lax.axis_size("chip")
    cols = lax.axis_size("col")
    half = width // cores
    own_blocks = own_rows // side
    col_blocks = own_blocks * cols
    row_blocks = own_blocks * cores * chips
    nodes = own_rows * cores * chips * cols
    core = lax.axis_index("core")

    swap = [(0, 1), (1, 0)]
    own = tiles[0, 0]
    sib = lax.ppermute(own, "core", swap)
    ids = jnp.stack(
        [
            tile_rows[0, 0],
            tile_cols[0, 0] + core * col_blocks,
            jnp.broadcast_to(tile_count[0, 0], (slots,)),
        ]
    )
    both = jnp.stack([ids, lax.ppermute(ids, "core", swap)])
    row_ids, col_ids, counts = both[:, 0], both[:, 1], both[:, 2, 0]

    halves = features.reshape(own_rows, cores, half).transpose(1, 0, 2)
    sent = jnp.broadcast_to(halves[:, None], (cores, cols, own_rows, half))
    sent = sent.reshape(cores * cols, own_rows, half)
    stripe = lax.all_to_all(sent, ("core", "col"), 0, 0, tiled=True)
    stripe = stripe.reshape(cores * col_blocks, side, half)
    partial_sums = tile_sums(True, counts, row_ids, col_ids, own, sib, stripe, row_blocks)
    partial_sums = partial_sums.reshape(chips * cores, own_rows, half)
    parts = lax.all_to_all(partial_sums, ("chip", "core"), 0, 0, tiled=True)
    act, grad, wgrad = middle(parts.reshape(chips, cores, own_rows, half), weight, cotangent)

    wgrad = lax.psum_scatter(wgrad, ("chip", "core"), scatter_dimension=0, tiled=True)
    wgrad = lax.psum(wgrad, "col") * float(nodes) ** (-0.5)
    wgrad = lax.all_gather(wgrad, ("chip", "core"), axis=0, tiled=True)

    grad = lax.all_to_all(
        grad.reshape(chips * cores, own_rows, half), ("chip", "core"), 0, 0, tiled=True
    )
    grad = grad.reshape(row_blocks, side, half)
    back = tile_sums(False, counts, row_ids, col_ids, own, sib, grad, cores * col_blocks)
    back = lax.all_to_all(
        back.reshape(cores * cols, own_rows, half), ("core", "col"), 0, 0, tiled=True
    )
    back = back.reshape(cores, cols, own_rows, half).astype(F32).sum(1).astype(BF)
    return act, wgrad, back.transpose(1, 0, 2).reshape(own_rows, width)


def solution(mesh):
    rows, cols = mesh.devices.shape
    fine = Mesh(mesh.devices.reshape(rows // 2, 2, cols), ("chip", "core", "col"))
    row = ("chip", "core")
    in_specs = (
        P((*row, "col"), None),
        P(),
        P(("col", *row), None),
        P(row, "col", None, None, None),
        P(row, "col", None),
        P(row, "col", None),
        P(row, "col", None),
    )
    out_specs = (P(("col", *row), None), P(), P((*row, "col"), None))
    return jax.shard_map(local, mesh=fine, in_specs=in_specs, out_specs=out_specs, check_vma=False)
```

```python
import jax
import jax.numpy as jnp
from jax import lax
from jax.experimental import pallas as pl
from jax.experimental.pallas import tpu as pltpu
from jax.sharding import Mesh, PartitionSpec as P

BF = jnp.bfloat16
F32 = jnp.float32
CHUNK = 64
UNROLL = 32


def tile_sums(forward, counts, rows, cols, own, sib, source, out_blocks):
    slots, side, _ = own.shape
    width = source.shape[-1]
    turns = slots // CHUNK

    def kernel(counts, rows, cols, own, sib, source, out, total):
        step = pl.program_id(0)

        @pl.when(step == 0)
        def _():
            total[...] = jnp.zeros_like(total)

        def chunk_sums(which, held, chunk):
            live = jnp.clip(counts[which] - chunk * CHUNK, 0, CHUNK)

            def one(place, carry):
                slot = chunk * CHUNK + place
                r, c = rows[which, slot], cols[which, slot]
                if forward:
                    total[r] += jnp.dot(held[place], source[c], preferred_element_type=F32)
                else:
                    total[c] += lax.dot_general(
                        held[place], source[r], (((0,), (0,)), ((), ())), preferred_element_type=F32
                    )
                return carry

            def several(group, carry):
                for u in range(UNROLL):
                    one(group * UNROLL + u, 0)
                return carry

            full = live // UNROLL
            lax.fori_loop(0, full, several, 0)
            lax.fori_loop(full * UNROLL, live, one, 0)

        @pl.when(step < turns)
        def _():
            chunk_sums(0, own, step)

        @pl.when(step >= turns)
        def _():
            chunk_sums(1, sib, step - turns)

        @pl.when(step == 2 * turns - 1)
        def _():
            out[...] = total[...].astype(BF)

    def own_at(i, counts, *_):
        return (jnp.minimum(jnp.minimum(i, turns - 1), jnp.maximum(counts[0] - 1, 0) // CHUNK), 0, 0)

    def sib_at(i, counts, *_):
        return (jnp.minimum(jnp.maximum(i - turns, 0), jnp.maximum(counts[1] - 1, 0) // CHUNK), 0, 0)

    shape = (out_blocks, side, width)
    return pl.pallas_call(
        kernel,
        grid_spec=pltpu.PrefetchScalarGridSpec(
            num_scalar_prefetch=3,
            grid=(2 * turns,),
            in_specs=[
                pl.BlockSpec((CHUNK, side, side), own_at),
                pl.BlockSpec((CHUNK, side, side), sib_at),
                pl.BlockSpec(source.shape, lambda i, *_: (0, 0, 0)),
            ],
            out_specs=pl.BlockSpec(shape, lambda i, *_: (0, 0, 0)),
            scratch_shapes=[pltpu.VMEM(shape, F32)],
        ),
        out_shape=jax.ShapeDtypeStruct(shape, BF),
        compiler_params=pltpu.CompilerParams(
            vmem_limit_bytes=40 << 20, dimension_semantics=("arbitrary",)
        ),
        cost_estimate=pl.CostEstimate(
            flops=4 * slots * side * side * width, bytes_accessed=16 << 20, transcendentals=0
        ),
        name="forward_tiles" if forward else "backward_tiles",
    )(counts, rows, cols, own, sib, source)


def middle(parts, weight, cotangent):
    chips, cores, own_rows, half = parts.shape
    width = cores * half
    share = width // (chips * cores)

    def kernel(parts, weight, cot, act, grad):
        w = weight[...]
        mixed = jnp.concatenate(
            [jnp.sum(parts[:, s].astype(F32), axis=0).astype(BF) for s in range(cores)], axis=1
        )
        pre = jnp.dot(mixed, w, preferred_element_type=F32)
        sig = jax.nn.sigmoid(pre)
        act[...] = (pre * sig).astype(BF)
        slope = sig * (1.0 + pre * (1.0 - sig))
        grad_pre = (cot[...].astype(F32) * slope).astype(BF)
        wgrad = lax.dot_general(
            mixed, grad_pre, (((0,), (0,)), ((), ())), preferred_element_type=F32
        ).astype(BF)
        mixed_grad = lax.dot_general(
            grad_pre, w, (((1,), (1,)), ((), ())), preferred_element_type=F32
        ).astype(BF)
        for s in range(cores):
            piece = mixed_grad[:, s * half : (s + 1) * half]
            for chip in range(chips):
                grad[chip, s, :own_rows] = piece
                at = (chip * cores + s) * share
                for h in range(cores):
                    grad[chip, s, own_rows + h * share : own_rows + (h + 1) * share] = wgrad[
                        at : at + share, h * half : (h + 1) * half
                    ]

    return pl.pallas_call(
        kernel,
        out_shape=(
            jax.ShapeDtypeStruct((own_rows, width), BF),
            jax.ShapeDtypeStruct((chips, cores, own_rows + cores * share, half), BF),
        ),
        compiler_params=pltpu.CompilerParams(vmem_limit_bytes=40 << 20),
        cost_estimate=pl.CostEstimate(
            flops=6 * own_rows * width * width, bytes_accessed=7 << 20, transcendentals=own_rows * width
        ),
        name="middle",
    )(parts, weight, cotangent)


def local(features, weight, cotangent, tiles, tile_rows, tile_cols, tile_count):
    slots, side = tiles.shape[2], tiles.shape[3]
    own_rows, width = features.shape
    cores = lax.axis_size("core")
    chips = lax.axis_size("chip")
    cols = lax.axis_size("col")
    half = width // cores
    own_blocks = own_rows // side
    col_blocks = own_blocks * cols
    row_blocks = own_blocks * cores * chips
    nodes = own_rows * cores * chips * cols
    core = lax.axis_index("core")

    swap = [(0, 1), (1, 0)]
    own = tiles[0, 0]
    sib = lax.ppermute(own, "core", swap)
    ids = jnp.stack(
        [
            tile_rows[0, 0],
            tile_cols[0, 0] + core * col_blocks,
            jnp.broadcast_to(tile_count[0, 0], (slots,)),
        ]
    )
    both = jnp.stack([ids, lax.ppermute(ids, "core", swap)])
    row_ids, col_ids, counts = both[:, 0], both[:, 1], both[:, 2, 0]

    halves = features.reshape(own_rows, cores, half).transpose(1, 0, 2)
    sent = jnp.broadcast_to(halves[:, None], (cores, cols, own_rows, half))
    sent = sent.reshape(cores * cols, own_rows, half)
    stripe = lax.all_to_all(sent, ("core", "col"), 0, 0, tiled=True)
    stripe = stripe.reshape(cores * col_blocks, side, half)
    partial_sums = tile_sums(True, counts, row_ids, col_ids, own, sib, stripe, row_blocks)
    partial_sums = partial_sums.reshape(chips * cores, own_rows, half)
    parts = lax.all_to_all(partial_sums, ("chip", "core"), 0, 0, tiled=True)
    act, grad = middle(parts.reshape(chips, cores, own_rows, half), weight, cotangent)

    exchanged = lax.all_to_all(
        grad.reshape(chips * cores, -1, half), ("chip", "core"), 0, 0, tiled=True
    )
    grad = exchanged[:, :own_rows].reshape(row_blocks, side, half)
    wgrad = exchanged[:, own_rows:].astype(F32).sum(0) * float(nodes) ** (-0.5)
    wgrad = jnp.broadcast_to(wgrad[None], (cols, *wgrad.shape))
    wgrad = lax.all_to_all(wgrad, "col", 0, 0, tiled=True).sum(0)
    wgrad = jnp.concatenate([wgrad[: wgrad.shape[0] // 2], wgrad[wgrad.shape[0] // 2 :]], axis=1)
    other = lax.ppermute(wgrad, "core", swap)
    wgrad = jnp.where(core == 0, jnp.concatenate([wgrad, other]), jnp.concatenate([other, wgrad]))
    chip = lax.axis_index("chip")
    gathered = jnp.zeros((chips, *wgrad.shape), F32)
    for away in range(chips):
        piece = wgrad
        if away:
            piece = lax.ppermute(wgrad, "chip", [(i, i ^ away) for i in range(chips)])
        gathered = lax.dynamic_update_slice(gathered, piece[None], (chip ^ away, 0, 0))
    wgrad = gathered.reshape(width, width)

    back = tile_sums(False, counts, row_ids, col_ids, own, sib, grad, cores * col_blocks)
    back = lax.all_to_all(
        back.reshape(cores * cols, own_rows, half), ("core", "col"), 0, 0, tiled=True
    )
    back = back.reshape(cores, cols, own_rows, half).astype(F32).sum(1).astype(BF)
    return act, wgrad, back.transpose(1, 0, 2).reshape(own_rows, width)


def solution(mesh):
    rows, cols = mesh.devices.shape
    fine = Mesh(mesh.devices.reshape(rows // 2, 2, cols), ("chip", "core", "col"))
    row = ("chip", "core")
    in_specs = (
        P((*row, "col"), None),
        P(),
        P(("col", *row), None),
        P(row, "col", None, None, None),
        P(row, "col", None),
        P(row, "col", None),
        P(row, "col", None),
    )
    out_specs = (P(("col", *row), None), P(), P((*row, "col"), None))
    return jax.shard_map(local, mesh=fine, in_specs=in_specs, out_specs=out_specs, check_vma=False)
```

```python
import jax
import jax.numpy as jnp
from jax import lax
from jax.experimental import pallas as pl
from jax.experimental.pallas import tpu as pltpu
from jax.sharding import Mesh, PartitionSpec as P

BF = jnp.bfloat16
F32 = jnp.float32
CHUNK = 32
RING = 4
ROW = ("x", "zl", "core")
COL = ("y", "zh")
VMEM = pl.BlockSpec(memory_space=pltpu.VMEM)
SMEM = pl.BlockSpec(memory_space=pltpu.SMEM)
PARAMS = pltpu.CompilerParams(vmem_limit_bytes=40 << 20)


def tile_sums(forward, ids, own, sib, source, out_blocks):
    slots, side, _ = own.shape
    width = source.shape[-1]
    shape = (out_blocks, side, width)
    turns = slots // CHUNK

    def kernel(ids, own, sib, source, out, total, *fetched):
        def fetch(which, ref, turn):
            held, sems = fetched
            chunk = pl.ds(turn * CHUNK, CHUNK)
            return pltpu.make_async_copy(
                ref.at[chunk], held.at[which, chunk], sems.at[which * turns + turn]
            )

        if fetched:
            for which, ref in enumerate((own, sib)):
                for turn in range(turns):

                    @pl.when(ids[which, 2, 0] > turn * CHUNK)
                    def _(which=which, ref=ref, turn=turn):
                        fetch(which, ref, turn).start()

        total[...] = jnp.zeros_like(total)

        def block(index):
            return source[index // 2, pl.ds(pl.multiple_of(index % 2 * side, side), side)]

        for which, ref in enumerate((own, sib)):
            held = fetched[0].at[which] if fetched else ref

            def one(slot, which=which, held=held):
                r, c = ids[which, 0, slot], ids[which, 1, slot]
                if forward:
                    total[r] += jnp.dot(held[slot], block(c), preferred_element_type=F32)
                else:
                    total[c] += lax.dot_general(
                        held[slot], block(r), (((0,), (0,)), ((), ())), preferred_element_type=F32
                    )

            count = ids[which, 2, 0]

            @pl.loop(0, turns)
            def _(turn, which=which, ref=ref, one=one, count=count):
                start = turn * CHUNK
                if fetched:

                    @pl.when(count > start)
                    def _():
                        fetch(which, ref, turn).wait()

                @pl.when(count >= start + CHUNK)
                def _():
                    for u in range(CHUNK):
                        one(start + u)

                @pl.when((count > start) & (count < start + CHUNK))
                def _():
                    @pl.loop(start, count)
                    def _(slot):
                        one(slot)

        out[...] = total[...].astype(BF)

    scratch = [pltpu.VMEM(shape, F32)]
    if not forward:
        scratch += [
            pltpu.VMEM((2, slots, side, side), BF),
            pltpu.SemaphoreType.DMA((2 * turns,)),
        ]
    place = VMEM if forward else pl.BlockSpec(memory_space=pltpu.HBM)
    return pl.pallas_call(
        kernel,
        in_specs=[SMEM, place, place, VMEM],
        out_specs=VMEM,
        scratch_shapes=scratch,
        out_shape=jax.ShapeDtypeStruct(shape, BF),
        compiler_params=PARAMS if forward else pltpu.CompilerParams(vmem_limit_bytes=60 << 20),
        cost_estimate=pl.CostEstimate(
            flops=4 * slots * side * side * width, bytes_accessed=16 << 20, transcendentals=0
        ),
        name="forward_tiles" if forward else "backward_tiles",
    )(ids, own, sib, source)


def spread(features, cols):
    rows, width = features.shape
    half = width // 2

    def kernel(source, out):
        for s in range(2):
            piece = source[:, s * half : (s + 1) * half]
            for c in range(cols):
                out[s * cols + c] = piece

    return pl.pallas_call(
        kernel,
        in_specs=[VMEM],
        out_specs=VMEM,
        out_shape=jax.ShapeDtypeStruct((2 * cols, rows, half), BF),
        compiler_params=PARAMS,
        name="spread",
    )(features)


def finish(spot, parts, own, sibling):
    many, rows, half = parts.shape
    aways, pairs, _, share, _ = own.shape

    def kernel(spot, parts, own, sibling, out, wgrad):
        for s in range(2):
            here = slice(s * half, (s + 1) * half)
            total = parts[s * (many // 2)].astype(F32)
            for c in range(1, many // 2):
                total += parts[s * (many // 2) + c].astype(F32)
            out[:, here] = total.astype(BF)
            for d in range(aways):
                for q in range(pairs):
                    for other, ref in enumerate((own, sibling)):
                        r = ((spot[1] ^ d) * pairs + q) * 2 + (spot[0] ^ other)
                        at = pl.multiple_of(r * share, share)
                        wgrad[pl.ds(at, share), here] = ref[d, q, s].astype(F32)

    return pl.pallas_call(
        kernel,
        in_specs=[SMEM, VMEM, VMEM, VMEM],
        out_specs=(VMEM, VMEM),
        out_shape=(
            jax.ShapeDtypeStruct((rows, 2 * half), BF),
            jax.ShapeDtypeStruct((2 * half, 2 * half), F32),
        ),
        compiler_params=PARAMS,
        name="finish",
    )(spot, parts, own, sibling)


def middle(parts, weight, cotangent):
    many, own_rows, half = parts.shape
    chips = many // 2
    width = 2 * half
    share = width // many

    def kernel(parts, weight, cot, act, grad):
        w = weight[...]
        mixed = []
        for s in range(2):
            total = parts[s].astype(F32)
            for chip in range(1, chips):
                total += parts[chip * 2 + s].astype(F32)
            mixed.append(total.astype(BF))
        mixed = jnp.concatenate(mixed, axis=1)
        pre = jnp.dot(mixed, w, preferred_element_type=F32)
        sig = jax.nn.sigmoid(pre)
        act[...] = (pre * sig).astype(BF)
        slope = sig * (1.0 + pre * (1.0 - sig))
        grad_pre = (cot[...].astype(F32) * slope).astype(BF)
        wgrad = lax.dot_general(
            mixed, grad_pre, (((0,), (0,)), ((), ())), preferred_element_type=F32
        ).astype(BF)
        mixed_grad = lax.dot_general(
            grad_pre, w, (((1,), (1,)), ((), ())), preferred_element_type=F32
        ).astype(BF)
        for s in range(2):
            piece = mixed_grad[:, s * half : (s + 1) * half]
            for chip in range(chips):
                to = chip * 2 + s
                grad[to, :own_rows] = piece
                for h in range(2):
                    first = own_rows + h * share
                    grad[to, first : first + share] = wgrad[
                        to * share : (to + 1) * share, h * half : (h + 1) * half
                    ]

    return pl.pallas_call(
        kernel,
        in_specs=[VMEM, VMEM, VMEM],
        out_specs=(VMEM, VMEM),
        out_shape=(
            jax.ShapeDtypeStruct((own_rows, width), BF),
            jax.ShapeDtypeStruct((many, own_rows + 2 * share, half), BF),
        ),
        compiler_params=PARAMS,
        cost_estimate=pl.CostEstimate(
            flops=6 * own_rows * width * width, bytes_accessed=7 << 20, transcendentals=own_rows * width
        ),
        name="middle",
    )(parts, weight, cotangent)


def exchange(array, axes):
    return lax.all_to_all(array, axes, 0, 0, tiled=True)


def copies(array, count):
    return jnp.broadcast_to(array[None], (count, *array.shape))


def local(features, weight, cotangent, tiles, tile_rows, tile_cols, tile_count):
    slots, side = tiles.shape[2], tiles.shape[3]
    own_rows, width = features.shape
    chips = lax.axis_size(("x", "zl"))
    cols = lax.axis_size(COL)
    half = width // 2
    own_blocks = own_rows // side
    col_blocks = own_blocks * cols
    row_blocks = own_blocks * 2 * chips
    nodes = own_rows * 2 * chips * cols
    core = lax.axis_index("core")
    swap = [(0, 1), (1, 0)]

    ids = jnp.stack(
        [
            tile_rows[0, 0],
            tile_cols[0, 0] + core * col_blocks,
            jnp.broadcast_to(tile_count[0, 0], (slots,)),
        ]
    )
    ids = jnp.stack([ids, lax.ppermute(ids, "core", swap)])
    sent, ids, own = lax.optimization_barrier((spread(features, cols), ids, tiles))
    own = own[0, 0]
    sib = lax.ppermute(own, "core", swap)

    stripe = exchange(sent, ("core", *COL))
    sums = tile_sums(True, ids, own, sib, stripe, row_blocks)
    parts = exchange(sums.reshape(2 * chips, own_rows, half), ROW)
    act, grad = middle(parts, weight, cotangent)
    grad = exchange(grad, ROW)

    wgrad = grad[:, own_rows:].astype(F32).sum(0) * float(nodes) ** (-0.5)
    wgrad = exchange(copies(wgrad.astype(BF), 2 * cols), ("zl", *COL))
    back = tile_sums(False, ids, own, sib, grad, 2 * col_blocks)
    back, wgrad = lax.optimization_barrier((back, wgrad))
    wgrad = wgrad.reshape(2, cols, 2, -1, half).astype(F32).sum(1).astype(BF)
    wgrad = jnp.stack(
        [wgrad]
        + [lax.ppermute(wgrad, "x", [(i, i ^ d) for i in range(RING)]) for d in range(1, RING)]
    )
    sibling = lax.ppermute(wgrad, "core", swap)
    back = exchange(back.reshape(2 * cols, own_rows, half), ("core", *COL))
    spot = jnp.stack([core, lax.axis_index("x")])
    feature_grad, wgrad = finish(spot, back, wgrad, sibling)
    return act, wgrad, feature_grad


def solution(mesh):
    rows, cols = mesh.devices.shape
    fine = Mesh(
        mesh.devices.reshape(RING, rows // (2 * RING), 2, RING, cols // RING),
        ("x", "zl", "core", "y", "zh"),
    )
    in_specs = (
        P((*ROW, *COL), None),
        P(),
        P((*COL, *ROW), None),
        P(ROW, COL, None, None, None),
        P(ROW, COL, None),
        P(ROW, COL, None),
        P(ROW, COL, None),
    )
    out_specs = (P((*COL, *ROW), None), P(), P((*ROW, *COL), None))
    return jax.shard_map(local, mesh=fine, in_specs=in_specs, out_specs=out_specs, check_vma=False)
```

```python
import jax
import jax.numpy as jnp
from jax import lax
from jax.experimental import pallas as pl
from jax.experimental.pallas import tpu as pltpu
from jax.sharding import Mesh, PartitionSpec as P

BF = jnp.bfloat16
F32 = jnp.float32
CHUNK = 32
RING = 4
ROW = ("x", "zl", "core")
COL = ("y", "zh")
VMEM = pl.BlockSpec(memory_space=pltpu.VMEM)
SMEM = pl.BlockSpec(memory_space=pltpu.SMEM)
PARAMS = pltpu.CompilerParams(vmem_limit_bytes=40 << 20)


def tile_sums(forward, ids, own, sib, source, out_blocks):
    slots, side, _ = own.shape
    width = source.shape[-1]
    shape = (out_blocks, side, width)

    def kernel(ids, own, sib, source, out, total):
        total[...] = jnp.zeros_like(total)

        def block(index):
            return source[index // 2, pl.ds(pl.multiple_of(index % 2 * side, side), side)]

        for which, held in enumerate((own, sib)):

            def one(slot, which=which, held=held):
                r, c = ids[which, 0, slot], ids[which, 1, slot]
                if forward:
                    total[r] += jnp.dot(held[slot], block(c), preferred_element_type=F32)
                else:
                    total[c] += lax.dot_general(
                        held[slot], block(r), (((0,), (0,)), ((), ())), preferred_element_type=F32
                    )

            count = ids[which, 2, 0]

            @pl.loop(0, slots // CHUNK)
            def _(turn, one=one, count=count):
                start = turn * CHUNK

                @pl.when(count >= start + CHUNK)
                def _():
                    for u in range(CHUNK):
                        one(start + u)

                @pl.when((count > start) & (count < start + CHUNK))
                def _():
                    @pl.loop(start, count)
                    def _(slot):
                        one(slot)

        out[...] = total[...].astype(BF)

    return pl.pallas_call(
        kernel,
        in_specs=[SMEM, VMEM, VMEM, VMEM],
        out_specs=VMEM,
        scratch_shapes=[pltpu.VMEM(shape, F32)],
        out_shape=jax.ShapeDtypeStruct(shape, BF),
        compiler_params=PARAMS,
        cost_estimate=pl.CostEstimate(
            flops=4 * slots * side * side * width, bytes_accessed=16 << 20, transcendentals=0
        ),
        name="forward_tiles" if forward else "backward_tiles",
    )(ids, own, sib, source)


def spread(features, cols):
    rows, width = features.shape
    half = width // 2

    def kernel(source, out):
        for s in range(2):
            piece = source[:, s * half : (s + 1) * half]
            for c in range(cols):
                out[s * cols + c] = piece

    return pl.pallas_call(
        kernel,
        in_specs=[VMEM],
        out_specs=VMEM,
        out_shape=jax.ShapeDtypeStruct((2 * cols, rows, half), BF),
        compiler_params=PARAMS,
        name="spread",
    )(features)


def column_sum(parts):
    many, rows, half = parts.shape

    def kernel(parts, out):
        for s in range(2):
            total = parts[s * (many // 2)].astype(F32)
            for c in range(1, many // 2):
                total += parts[s * (many // 2) + c].astype(F32)
            out[:, s * half : (s + 1) * half] = total.astype(BF)

    return pl.pallas_call(
        kernel,
        in_specs=[VMEM],
        out_specs=VMEM,
        out_shape=jax.ShapeDtypeStruct((rows, 2 * half), BF),
        compiler_params=PARAMS,
        name="column_sum",
    )(parts)


def place_shares(spot, own, sibling):
    aways, pairs, _, share, half = own.shape

    def kernel(spot, own, sibling, wgrad):
        for s in range(2):
            here = slice(s * half, (s + 1) * half)
            for d in range(aways):
                for q in range(pairs):
                    for other, ref in enumerate((own, sibling)):
                        r = ((spot[1] ^ d) * pairs + (spot[2] ^ q)) * 2 + (spot[0] ^ other)
                        at = pl.multiple_of(r * share, share)
                        wgrad[pl.ds(at, share), here] = ref[d, q, s].astype(F32)

    return pl.pallas_call(
        kernel,
        in_specs=[SMEM, VMEM, VMEM],
        out_specs=VMEM,
        out_shape=jax.ShapeDtypeStruct((2 * half, 2 * half), F32),
        compiler_params=PARAMS,
        cost_estimate=pl.CostEstimate(flops=0, bytes_accessed=2 << 20, transcendentals=0),
        name="place_shares",
    )(spot, own, sibling)


def middle(parts, weight, cotangent):
    many, own_rows, half = parts.shape
    chips = many // 2
    width = 2 * half
    share = width // many

    def kernel(parts, weight, cot, act, grad):
        w = weight[...]
        mixed = []
        for s in range(2):
            total = parts[s].astype(F32)
            for chip in range(1, chips):
                total += parts[chip * 2 + s].astype(F32)
            mixed.append(total.astype(BF))
        mixed = jnp.concatenate(mixed, axis=1)
        pre = jnp.dot(mixed, w, preferred_element_type=F32)
        sig = jax.nn.sigmoid(pre)
        act[...] = (pre * sig).astype(BF)
        slope = sig * (1.0 + pre * (1.0 - sig))
        grad_pre = (cot[...].astype(F32) * slope).astype(BF)
        wgrad = lax.dot_general(
            mixed, grad_pre, (((0,), (0,)), ((), ())), preferred_element_type=F32
        ).astype(BF)
        mixed_grad = lax.dot_general(
            grad_pre, w, (((1,), (1,)), ((), ())), preferred_element_type=F32
        ).astype(BF)
        for s in range(2):
            piece = mixed_grad[:, s * half : (s + 1) * half]
            for chip in range(chips):
                to = chip * 2 + s
                grad[to, :own_rows] = piece
                for h in range(2):
                    first = own_rows + h * share
                    grad[to, first : first + share] = wgrad[
                        to * share : (to + 1) * share, h * half : (h + 1) * half
                    ]

    return pl.pallas_call(
        kernel,
        in_specs=[VMEM, VMEM, VMEM],
        out_specs=(VMEM, VMEM),
        out_shape=(
            jax.ShapeDtypeStruct((own_rows, width), BF),
            jax.ShapeDtypeStruct((many, own_rows + 2 * share, half), BF),
        ),
        compiler_params=PARAMS,
        cost_estimate=pl.CostEstimate(
            flops=6 * own_rows * width * width, bytes_accessed=7 << 20, transcendentals=own_rows * width
        ),
        name="middle",
    )(parts, weight, cotangent)


def flip(array, axis, by=1):
    size = RING if axis in ("x", "y") else 2
    return lax.ppermute(array, axis, [(i, i ^ by) for i in range(size)])


def exchange(array, axes):
    return lax.all_to_all(array, axes, 0, 0, tiled=True)


def copies(array, count):
    return jnp.broadcast_to(array[None], (count, *array.shape))


def local(features, weight, cotangent, tiles, tile_rows, tile_cols, tile_count):
    slots, side = tiles.shape[2], tiles.shape[3]
    own_rows, width = features.shape
    chips = lax.axis_size(("x", "zl"))
    cols = lax.axis_size(COL)
    half = width // 2
    own_blocks = own_rows // side
    col_blocks = own_blocks * cols
    row_blocks = own_blocks * 2 * chips
    nodes = own_rows * 2 * chips * cols
    core = lax.axis_index("core")
    swap = [(0, 1), (1, 0)]

    ids = jnp.stack(
        [
            tile_rows[0, 0],
            tile_cols[0, 0] + core * col_blocks,
            jnp.broadcast_to(tile_count[0, 0], (slots,)),
        ]
    )
    ids = jnp.stack([ids, lax.ppermute(ids, "core", swap)])
    sent, ids, own = lax.optimization_barrier((spread(features, cols), ids, tiles))
    own = own[0, 0]
    sib = lax.ppermute(own, "core", swap)

    stripe = exchange(sent, ("core", *COL))
    sums = tile_sums(True, ids, own, sib, stripe, row_blocks)
    parts = exchange(sums.reshape(2 * chips, own_rows, half), ROW)
    act, grad = middle(parts, weight, cotangent)
    grad = exchange(grad, ROW)

    wgrad = grad[:, own_rows:].astype(F32).sum(0) * float(nodes) ** (-0.5)
    near, *far = (flip(wgrad, "y", d) for d in range(1, RING))
    back = tile_sums(False, ids, own, sib, grad, 2 * col_blocks)
    back, near, far = lax.optimization_barrier((back, near, far))
    wgrad = (wgrad + near) + (far[0] + far[1])
    across = lax.ppermute(wgrad, ("zl", "zh"), [(i, 3 - i) for i in range(4)])
    wgrad = jnp.stack([wgrad + flip(wgrad, "zh"), flip(wgrad, "zl") + across])
    wgrad = wgrad.reshape(2, 2, -1, half).astype(BF)
    wgrad = jnp.stack([wgrad, *(flip(wgrad, "x", d) for d in range(1, RING))])
    sibling = flip(wgrad, "core")
    back = exchange(back.reshape(2 * cols, own_rows, half), ("core", *COL))
    spot = jnp.stack([core, lax.axis_index("x"), lax.axis_index("zl")])
    return act, place_shares(spot, wgrad, sibling), column_sum(back)


def solution(mesh):
    rows, cols = mesh.devices.shape
    fine = Mesh(
        mesh.devices.reshape(RING, rows // (2 * RING), 2, RING, cols // RING),
        ("x", "zl", "core", "y", "zh"),
    )
    in_specs = (
        P((*ROW, *COL), None),
        P(),
        P((*COL, *ROW), None),
        P(ROW, COL, None, None, None),
        P(ROW, COL, None),
        P(ROW, COL, None),
        P(ROW, COL, None),
    )
    out_specs = (P((*COL, *ROW), None), P(), P((*ROW, *COL), None))
    return jax.shard_map(local, mesh=fine, in_specs=in_specs, out_specs=out_specs, check_vma=False)
```

```python
import jax
import jax.numpy as jnp
from jax import lax
from jax.experimental import pallas as pl
from jax.experimental.pallas import tpu as pltpu
from jax.sharding import Mesh, PartitionSpec as P

BF = jnp.bfloat16
F32 = jnp.float32
SIZES = (64, 16, 1)
RING = 4
ROW = ("x", "zl", "core")
COL = ("y", "zh")
ROW_ORDER = ("zl", "x", "core")
COL_ORDER = ("zh", "y", "core")
VMEM = pl.BlockSpec(memory_space=pltpu.VMEM)
SMEM = pl.BlockSpec(memory_space=pltpu.SMEM)
PARAMS = pltpu.CompilerParams(vmem_limit_bytes=40 << 20)


def tile_sums(forward, ids, own, sib, source, out_blocks):
    slots, side, _ = own.shape
    width = source.shape[-1]
    shape = (out_blocks, side, width)

    def kernel(ids, own, sib, source, out, total):
        total[...] = jnp.zeros_like(total)

        def block(index):
            return source[index // 2, pl.ds(pl.multiple_of(index % 2 * side, side), side)]

        for which, held in enumerate((own, sib)):

            def one(slot, which=which, held=held):
                r, c = ids[which, 0, slot], ids[which, 1 if forward else 3, slot]
                if forward:
                    total[r] += jnp.dot(held[slot], block(c), preferred_element_type=F32)
                else:
                    total[c] += lax.dot_general(
                        held[slot], block(r), (((0,), (0,)), ((), ())), preferred_element_type=F32
                    )

            count = ids[which, 2, 0]

            done = 0
            for size in SIZES:

                @pl.loop(done // size, count // size)
                def _(group, one=one, size=size):
                    for u in range(size):
                        one(group * size + u)

                done = count // size * size

        out[...] = total[...].astype(BF)

    return pl.pallas_call(
        kernel,
        in_specs=[SMEM, VMEM, VMEM, VMEM],
        out_specs=VMEM,
        scratch_shapes=[pltpu.VMEM(shape, F32)],
        out_shape=jax.ShapeDtypeStruct(shape, BF),
        compiler_params=PARAMS,
        cost_estimate=pl.CostEstimate(
            flops=4 * slots * side * side * width, bytes_accessed=16 << 20, transcendentals=0
        ),
        name="forward_tiles" if forward else "backward_tiles",
    )(ids, own, sib, source)


def spread(features, cols):
    rows, width = features.shape
    half = width // 2

    def kernel(source, out):
        for s in range(2):
            piece = source[:, s * half : (s + 1) * half]
            for c in range(cols):
                out[c * 2 + s] = piece

    return pl.pallas_call(
        kernel,
        in_specs=[VMEM],
        out_specs=VMEM,
        out_shape=jax.ShapeDtypeStruct((2 * cols, rows, half), BF),
        compiler_params=PARAMS,
        name="spread",
    )(features)


def column_sum(parts):
    many, rows, half = parts.shape

    def kernel(parts, out):
        for s in range(2):
            total = parts[s * (many // 2)].astype(F32)
            for c in range(1, many // 2):
                total += parts[s * (many // 2) + c].astype(F32)
            out[:, s * half : (s + 1) * half] = total.astype(BF)

    return pl.pallas_call(
        kernel,
        in_specs=[VMEM],
        out_specs=VMEM,
        out_shape=jax.ShapeDtypeStruct((rows, 2 * half), BF),
        compiler_params=PARAMS,
        name="column_sum",
    )(parts)


def place_shares(spot, own, sibling):
    aways, pairs, _, share, half = own.shape

    def kernel(spot, own, sibling, wgrad):
        for s in range(2):
            here = slice(s * half, (s + 1) * half)
            for d in range(aways):
                for q in range(pairs):
                    for other, ref in enumerate((own, sibling)):
                        r = ((spot[2] ^ q) * aways + (spot[1] ^ d)) * 2 + (spot[0] ^ other)
                        at = pl.multiple_of(r * share, share)
                        wgrad[pl.ds(at, share), here] = ref[d, q, s].astype(F32)

    return pl.pallas_call(
        kernel,
        in_specs=[SMEM, VMEM, VMEM],
        out_specs=VMEM,
        out_shape=jax.ShapeDtypeStruct((2 * half, 2 * half), F32),
        compiler_params=PARAMS,
        cost_estimate=pl.CostEstimate(flops=0, bytes_accessed=2 << 20, transcendentals=0),
        name="place_shares",
    )(spot, own, sibling)


def middle(parts, weight, cotangent):
    many, own_rows, half = parts.shape
    chips = many // 2
    width = 2 * half
    share = width // many

    def kernel(parts, weight, cot, act, grad):
        w = weight[...]
        mixed = []
        for s in range(2):
            total = parts[s].astype(F32)
            for chip in range(1, chips):
                total += parts[chip * 2 + s].astype(F32)
            mixed.append(total.astype(BF))
        mixed = jnp.concatenate(mixed, axis=1)
        pre = jnp.dot(mixed, w, preferred_element_type=F32)
        sig = jax.nn.sigmoid(pre)
        act[...] = (pre * sig).astype(BF)
        slope = sig * (1.0 + pre * (1.0 - sig))
        grad_pre = (cot[...].astype(F32) * slope).astype(BF)
        wgrad = lax.dot_general(
            mixed, grad_pre, (((0,), (0,)), ((), ())), preferred_element_type=F32
        ).astype(BF)
        mixed_grad = lax.dot_general(
            grad_pre, w, (((1,), (1,)), ((), ())), preferred_element_type=F32
        ).astype(BF)
        for s in range(2):
            piece = mixed_grad[:, s * half : (s + 1) * half]
            for chip in range(chips):
                to = chip * 2 + s
                grad[to, :own_rows] = piece
                for h in range(2):
                    first = own_rows + h * share
                    grad[to, first : first + share] = wgrad[
                        to * share : (to + 1) * share, h * half : (h + 1) * half
                    ]

    return pl.pallas_call(
        kernel,
        in_specs=[VMEM, VMEM, VMEM],
        out_specs=(VMEM, VMEM),
        out_shape=(
            jax.ShapeDtypeStruct((own_rows, width), BF),
            jax.ShapeDtypeStruct((many, own_rows + 2 * share, half), BF),
        ),
        compiler_params=PARAMS,
        cost_estimate=pl.CostEstimate(
            flops=6 * own_rows * width * width, bytes_accessed=7 << 20, transcendentals=own_rows * width
        ),
        name="middle",
    )(parts, weight, cotangent)


def flip(array, axis, by=1):
    size = RING if axis in ("x", "y") else 2
    return lax.ppermute(array, axis, [(i, i ^ by) for i in range(size)])


def exchange(array, axes):
    return lax.all_to_all(array, axes, 0, 0, tiled=True)


def copies(array, count):
    return jnp.broadcast_to(array[None], (count, *array.shape))


def local(features, weight, cotangent, tiles, tile_rows, tile_cols, tile_count):
    slots, side = tiles.shape[2], tiles.shape[3]
    own_rows, width = features.shape
    chips = lax.axis_size(("x", "zl"))
    cols = lax.axis_size(COL)
    half = width // 2
    own_blocks = own_rows // side
    col_blocks = own_blocks * cols
    row_blocks = own_blocks * 2 * chips
    nodes = own_rows * 2 * chips * cols
    core = lax.axis_index("core")
    swap = [(0, 1), (1, 0)]


    def entry(chip, core):
        return (chip % 2 * RING + chip // 2) * 2 + core

    ids = jnp.stack(
        [
            entry(tile_rows[0, 0] // 4, tile_rows[0, 0] // 2 % 2) * own_blocks + tile_rows[0, 0] % 2,
            entry(tile_cols[0, 0] // 2, core) * own_blocks + tile_cols[0, 0] % 2,
            jnp.broadcast_to(tile_count[0, 0], (slots,)),
            tile_cols[0, 0] + core * col_blocks,
        ]
    )
    ids = jnp.stack([ids, lax.ppermute(ids, "core", swap)])
    sent, ids, own = lax.optimization_barrier((spread(features, cols), ids, tiles))
    own = own[0, 0]
    sib = lax.ppermute(own, "core", swap)

    stripe = exchange(sent, COL_ORDER)
    sums = tile_sums(True, ids, own, sib, stripe, row_blocks)
    parts = exchange(sums.reshape(2 * chips, own_rows, half), ROW_ORDER)
    act, grad = middle(parts, weight, cotangent)
    grad = exchange(grad, ROW_ORDER)

    wgrad = grad[:, own_rows:].astype(F32).sum(0) * float(nodes) ** (-0.5)
    near, *far = (flip(wgrad, "y", d) for d in range(1, RING))
    back = tile_sums(False, ids, own, sib, grad, 2 * col_blocks)
    back, near, far = lax.optimization_barrier((back, near, far))
    wgrad = (wgrad + near) + (far[0] + far[1])
    across = lax.ppermute(wgrad, ("zl", "zh"), [(i, 3 - i) for i in range(4)])
    wgrad = jnp.stack([wgrad + flip(wgrad, "zh"), flip(wgrad, "zl") + across])
    wgrad = wgrad.reshape(2, 2, -1, half).astype(BF)
    wgrad = jnp.stack([wgrad, *(flip(wgrad, "x", d) for d in range(1, RING))])
    sibling = flip(wgrad, "core")
    back = exchange(back.reshape(2 * cols, own_rows, half), ("core", *COL))
    spot = jnp.stack([core, lax.axis_index("x"), lax.axis_index("zl")])
    return act, place_shares(spot, wgrad, sibling), column_sum(back)


def solution(mesh):
    rows, cols = mesh.devices.shape
    fine = Mesh(
        mesh.devices.reshape(RING, rows // (2 * RING), 2, RING, cols // RING),
        ("x", "zl", "core", "y", "zh"),
    )
    in_specs = (
        P((*ROW, *COL), None),
        P(),
        P((*COL, *ROW), None),
        P(ROW, COL, None, None, None),
        P(ROW, COL, None),
        P(ROW, COL, None),
        P(ROW, COL, None),
    )
    out_specs = (P((*COL, *ROW), None), P(), P((*ROW, *COL), None))
    return jax.shard_map(local, mesh=fine, in_specs=in_specs, out_specs=out_specs, check_vma=False)
```

```python
import jax
import jax.numpy as jnp
from jax import lax
from jax.experimental import pallas as pl
from jax.experimental.pallas import tpu as pltpu
from jax.sharding import Mesh, PartitionSpec as P

BF = jnp.bfloat16
F32 = jnp.float32
SIZES = (64, 32, 8, 1)
RING = 4
ROW = ("x", "zl", "core")
COL = ("y", "zh")
ROW_ORDER = ("zl", "x", "core")
COL_ORDER = ("zh", "y", "core")
VMEM = pl.BlockSpec(memory_space=pltpu.VMEM)
SMEM = pl.BlockSpec(memory_space=pltpu.SMEM)
PARAMS = pltpu.CompilerParams(vmem_limit_bytes=40 << 20)


def tile_sums(forward, ids, own, sib, source, out_blocks):
    slots, side, _ = own.shape
    width = source.shape[-1]
    shape = (out_blocks, side, width)

    def kernel(ids, own, sib, source, out, total):
        total[...] = jnp.zeros_like(total)

        def block(index):
            return source[index // 2, pl.ds(pl.multiple_of(index % 2 * side, side), side)]

        for which, held in enumerate((own, sib)):

            def one(slot, which=which, held=held):
                r, c = ids[which, 0, slot], ids[which, 1 if forward else 3, slot]
                if forward:
                    total[r] += jnp.dot(held[slot], block(c), preferred_element_type=F32)
                else:
                    total[c] += lax.dot_general(
                        held[slot], block(r), (((0,), (0,)), ((), ())), preferred_element_type=F32
                    )

            count = ids[which, 2, 0]

            done = 0
            for size in SIZES:

                @pl.loop(done // size, count // size)
                def _(group, one=one, size=size):
                    for u in range(size):
                        one(group * size + u)

                done = count // size * size

        out[...] = total[...].astype(BF)

    return pl.pallas_call(
        kernel,
        in_specs=[SMEM, VMEM, VMEM, VMEM],
        out_specs=VMEM,
        scratch_shapes=[pltpu.VMEM(shape, F32)],
        out_shape=jax.ShapeDtypeStruct(shape, BF),
        compiler_params=PARAMS,
        cost_estimate=pl.CostEstimate(
            flops=4 * slots * side * side * width, bytes_accessed=16 << 20, transcendentals=0
        ),
        name="forward_tiles" if forward else "backward_tiles",
    )(ids, own, sib, source)


def spread(features, cols):
    rows, width = features.shape
    half = width // 2

    def kernel(source, out):
        for s in range(2):
            piece = source[:, s * half : (s + 1) * half]
            for c in range(cols):
                out[c * 2 + s] = piece

    return pl.pallas_call(
        kernel,
        in_specs=[VMEM],
        out_specs=VMEM,
        out_shape=jax.ShapeDtypeStruct((2 * cols, rows, half), BF),
        compiler_params=PARAMS,
        name="spread",
    )(features)


def column_sum(parts):
    many, rows, half = parts.shape

    def kernel(parts, out):
        for s in range(2):
            total = parts[s * (many // 2)].astype(F32)
            for c in range(1, many // 2):
                total += parts[s * (many // 2) + c].astype(F32)
            out[:, s * half : (s + 1) * half] = total.astype(BF)

    return pl.pallas_call(
        kernel,
        in_specs=[VMEM],
        out_specs=VMEM,
        out_shape=jax.ShapeDtypeStruct((rows, 2 * half), BF),
        compiler_params=PARAMS,
        name="column_sum",
    )(parts)


def place_shares(spot, own, sibling):
    aways, pairs, _, share, half = own.shape

    def kernel(spot, own, sibling, wgrad):
        for s in range(2):
            here = slice(s * half, (s + 1) * half)
            for d in range(aways):
                for q in range(pairs):
                    for other, ref in enumerate((own, sibling)):
                        r = ((spot[2] ^ q) * aways + (spot[1] ^ d)) * 2 + (spot[0] ^ other)
                        at = pl.multiple_of(r * share, share)
                        wgrad[pl.ds(at, share), here] = ref[d, q, s].astype(F32)

    return pl.pallas_call(
        kernel,
        in_specs=[SMEM, VMEM, VMEM],
        out_specs=VMEM,
        out_shape=jax.ShapeDtypeStruct((2 * half, 2 * half), F32),
        compiler_params=PARAMS,
        cost_estimate=pl.CostEstimate(flops=0, bytes_accessed=2 << 20, transcendentals=0),
        name="place_shares",
    )(spot, own, sibling)


def middle(parts, weight, cotangent):
    many, own_rows, half = parts.shape
    chips = many // 2
    width = 2 * half
    share = width // many

    def kernel(parts, weight, cot, act, grad):
        w = weight[...]
        mixed = []
        for s in range(2):
            total = parts[s].astype(F32)
            for chip in range(1, chips):
                total += parts[chip * 2 + s].astype(F32)
            mixed.append(total.astype(BF))
        mixed = jnp.concatenate(mixed, axis=1)
        pre = jnp.dot(mixed, w, preferred_element_type=F32)
        sig = jax.nn.sigmoid(pre)
        act[...] = (pre * sig).astype(BF)
        slope = sig * (1.0 + pre * (1.0 - sig))
        grad_pre = (cot[...].astype(F32) * slope).astype(BF)
        wgrad = lax.dot_general(
            mixed, grad_pre, (((0,), (0,)), ((), ())), preferred_element_type=F32
        ).astype(BF)
        mixed_grad = lax.dot_general(
            grad_pre, w, (((1,), (1,)), ((), ())), preferred_element_type=F32
        ).astype(BF)
        for s in range(2):
            piece = mixed_grad[:, s * half : (s + 1) * half]
            for chip in range(chips):
                to = chip * 2 + s
                grad[to, :own_rows] = piece
                for h in range(2):
                    first = own_rows + h * share
                    grad[to, first : first + share] = wgrad[
                        to * share : (to + 1) * share, h * half : (h + 1) * half
                    ]

    return pl.pallas_call(
        kernel,
        in_specs=[VMEM, VMEM, VMEM],
        out_specs=(VMEM, VMEM),
        out_shape=(
            jax.ShapeDtypeStruct((own_rows, width), BF),
            jax.ShapeDtypeStruct((many, own_rows + 2 * share, half), BF),
        ),
        compiler_params=PARAMS,
        cost_estimate=pl.CostEstimate(
            flops=6 * own_rows * width * width, bytes_accessed=7 << 20, transcendentals=own_rows * width
        ),
        name="middle",
    )(parts, weight, cotangent)


def flip(array, axis, by=1):
    size = RING if axis in ("x", "y") else 2
    return lax.ppermute(array, axis, [(i, i ^ by) for i in range(size)])


def exchange(array, axes):
    return lax.all_to_all(array, axes, 0, 0, tiled=True)


def copies(array, count):
    return jnp.broadcast_to(array[None], (count, *array.shape))


def local(features, weight, cotangent, tiles, tile_rows, tile_cols, tile_count):
    slots, side = tiles.shape[2], tiles.shape[3]
    own_rows, width = features.shape
    chips = lax.axis_size(("x", "zl"))
    cols = lax.axis_size(COL)
    half = width // 2
    own_blocks = own_rows // side
    col_blocks = own_blocks * cols
    row_blocks = own_blocks * 2 * chips
    nodes = own_rows * 2 * chips * cols
    core = lax.axis_index("core")
    swap = [(0, 1), (1, 0)]


    def entry(chip, core):
        return (chip % 2 * RING + chip // 2) * 2 + core

    ids = jnp.stack(
        [
            entry(tile_rows[0, 0] // 4, tile_rows[0, 0] // 2 % 2) * own_blocks + tile_rows[0, 0] % 2,
            entry(tile_cols[0, 0] // 2, core) * own_blocks + tile_cols[0, 0] % 2,
            jnp.broadcast_to(tile_count[0, 0], (slots,)),
            tile_cols[0, 0] + core * col_blocks,
        ]
    )
    ids = jnp.stack([ids, lax.ppermute(ids, "core", swap)])
    sent, ids, own = lax.optimization_barrier((spread(features, cols), ids, tiles))
    own = own[0, 0]
    sib = lax.ppermute(own, "core", swap)

    stripe = exchange(sent, COL_ORDER)
    sums = tile_sums(True, ids, own, sib, stripe, row_blocks)
    parts = exchange(sums.reshape(2 * chips, own_rows, half), ROW_ORDER)
    act, grad = middle(parts, weight, cotangent)
    grad = exchange(grad, ROW_ORDER)

    wgrad = grad[:, own_rows:].astype(F32).sum(0) * float(nodes) ** (-0.5)
    near, *far = (flip(wgrad, "y", d) for d in range(1, RING))
    back = tile_sums(False, ids, own, sib, grad, 2 * col_blocks)
    back, near, far = lax.optimization_barrier((back, near, far))
    wgrad = (wgrad + near) + (far[0] + far[1])
    across = lax.ppermute(wgrad, ("zl", "zh"), [(i, 3 - i) for i in range(4)])
    wgrad = jnp.stack([wgrad + flip(wgrad, "zh"), flip(wgrad, "zl") + across])
    wgrad = wgrad.reshape(2, 2, -1, half).astype(BF)
    wgrad = jnp.stack([wgrad, *(flip(wgrad, "x", d) for d in range(1, RING))])
    sibling = flip(wgrad, "core")
    back = exchange(back.reshape(2 * cols, own_rows, half), ("core", *COL))
    spot = jnp.stack([core, lax.axis_index("x"), lax.axis_index("zl")])
    return act, place_shares(spot, wgrad, sibling), column_sum(back)


def solution(mesh):
    rows, cols = mesh.devices.shape
    fine = Mesh(
        mesh.devices.reshape(RING, rows // (2 * RING), 2, RING, cols // RING),
        ("x", "zl", "core", "y", "zh"),
    )
    in_specs = (
        P((*ROW, *COL), None),
        P(),
        P((*COL, *ROW), None),
        P(ROW, COL, None, None, None),
        P(ROW, COL, None),
        P(ROW, COL, None),
        P(ROW, COL, None),
    )
    out_specs = (P((*COL, *ROW), None), P(), P((*ROW, *COL), None))
    return jax.shard_map(local, mesh=fine, in_specs=in_specs, out_specs=out_specs, check_vma=False)
```
